32 devices in a mesh: dp: 8 (over y, x, core), seq: 4 (over z).
Axes of the slice: x: 2, y: 2, z: 4, core: 2. Of those that a mesh axis runs over, the one named last changes fastest.
Arguments:
- grad_out: bfloat16 [4096, 1280], P(('dp', 'seq')), may hold values from -6 to 6
- saved_input: bfloat16 [4096, 1280], P(('dp', 'seq')), may hold values from -6 to 6
- pre_glu: bfloat16 [4096, 2560], P(('dp', 'seq')), may hold values from -6 to 6
- queries: bfloat16 [4096, 1280], P('dp', 'seq'), may hold values from -8 to 8
- keys: bfloat16 [4096, 1280], P('dp', 'seq'), may hold values from -8 to 8
- values: bfloat16 [4096, 1280], P('dp', 'seq'), may hold values from -6 to 6
- frame_counts: int32 [8, 8], P('dp'), may hold values from 1 to 256, 512 in all within a row
- norm_gain: float32 [1280], replicated, may hold values from 0.5 to 1.5
- kernel: float32 [31, 1280], replicated, may hold values from -1 to 1
- w_in: bfloat16 [1280, 2560], P('dp'), may hold values from -0.15625 to 0.15625
- w_conv_out: bfloat16 [1280, 1280], P('dp'), may hold values from -0.15625 to 0.15625
- w_attn_out: bfloat16 [1280, 1280], P('dp'), may hold values from -0.15625 to 0.15625
Outputs:
- resid_grad: bfloat16 [4096, 1280], P(('dp', 'seq'))
- query_grad: bfloat16 [4096, 1280], P('dp', 'seq')
- key_grad: bfloat16 [4096, 1280], P('dp', 'seq')
- value_grad: bfloat16 [4096, 1280], P('dp', 'seq')
- kernel_grad: float32 [31, 1280], replicated
- gain_grad: float32 [1280], replicated
The draws below stay inside these ranges and needn't reach their ends.
Inputs may be any that keep to these rules, and one draw needn't show every extreme that they name: `frame_counts`: each row sums to 512; its largest entry is exactly 256.
All inputs are finite; a program needn't handle non-finite values.
Results may differ from the reference program's by a relative error of at most 0.018.
Values may be sent and summed in bfloat16 or wider, within the bound.
A program may use at most 64 MiB of HBM per device.

```python
import math
import jax
import jax.numpy as jnp
import numpy as np
from jax import lax

D = 1280
H = 16
HD = 80
KW = 31
UTTS = 8
TOTAL = 512
FRAMES = 4096
MOST = 256
N_DP = 8


def drawn_pair(key):
    base = jax.random.fold_in(key, 11)
    query_key, other_key = jax.random.split(base, 2)
    query = jnp.clip(jax.random.normal(query_key, (FRAMES, D), jnp.float32), -6.0, 6.0)
    keyset = jnp.clip(jax.random.normal(other_key, (FRAMES, D), jnp.float32), -6.0, 6.0)
    return (query, keyset)


def draw_queries(key, part):
    return drawn_pair(key)[0].astype(jnp.bfloat16)


def draw_keys(key, part):
    return drawn_pair(key)[1].astype(jnp.bfloat16)


def levels(key, shape, cuts, smallest, high):
    level = 1.0
    for dim, parts in cuts:
        steps = jax.random.uniform(jax.random.fold_in(jax.random.fold_in(key, 6), dim), (parts,), jnp.float32, smallest / len(cuts), high / len(cuts))
        level = level * jnp.repeat(jnp.exp(steps), shape[dim] // parts).reshape((-1,) + (1,) * (len(shape) - 1 - dim))
    return level


def profile(count, total, reach, lean):
    portions = [(1 << 20) // math.isqrt(rank ** lean) + 1 for rank in range(2, count + 1)]
    spare, holding = total - reach - (count - 1), [1] * (count - 1)
    while spare > 0:
        free = [i for i in range(count - 1) if holding[i] < reach]
        mass, budget = sum([portions[i] for i in free]), spare
        for i in free:
            more = min(reach - holding[i], max(1, budget * portions[i] // mass), spare)
            holding[i] = holding[i] + more
            spare = spare - more
    return np.array([reach] + holding)


def uneven(key, number_of, total, bound, lean):
    if number_of == 2:
        one = jax.random.randint(key, (), max(1, total - bound), min(bound, total - 1) + 1)
        return jnp.stack([one, total - one])
    lengths = jnp.asarray(profile(number_of, total, bound, lean), jnp.int32)
    couples = (number_of - 1) // 2
    source_of, receiver = lengths[1:1 + 2 * couples:2], lengths[2:2 + 2 * couples:2]
    margin = jnp.minimum(source_of - 1, bound - receiver)
    shifted = jax.random.randint(jax.random.fold_in(key, 1), (couples,), 0, 1 << 20) % (margin + 1)
    lengths = lengths.at[1:1 + 2 * couples:2].set(source_of - shifted).at[2:2 + 2 * couples:2].set(receiver + shifted)
    return lengths[jax.random.permutation(jax.random.fold_in(key, 2), number_of)]


def scatter_about(own_key, shape, scale, most, cuts=(), kind=jnp.bfloat16):
    level = levels(own_key, shape, cuts, -0.22, 0.18) if cuts else 1.0
    result = jax.random.normal(own_key, shape, jnp.float32) * scale * level
    return jnp.minimum(jnp.maximum(result, -most), most).astype(kind)


def setup_inputs(seed: int = 0) -> dict:
    splits = jax.random.split(jax.random.key(seed), 13)
    grad_out = scatter_about(splits[0], (FRAMES, D), 1.0, 6.0, ((0, 32),))
    saved_input = scatter_about(splits[1], (FRAMES, D), 1.0, 6.0, ((0, 32),))
    pre_glu = scatter_about(splits[2], (FRAMES, 2 * D), 1.0, 6.0, ((0, 32),))
    queries = draw_queries(jax.random.fold_in(splits[12], 71), 0)
    keys = draw_keys(jax.random.fold_in(splits[12], 71), 0)
    values = scatter_about(splits[5], (FRAMES, D), 1.0, 6.0, ((0, 8), (1, 4)))
    frame_counts = jax.vmap(lambda own: uneven(own, UTTS, TOTAL, MOST, 2))(jax.random.split(splits[6], N_DP)).reshape((N_DP, UTTS)).astype(jnp.int32)
    norm_gain = jnp.clip(1.0 + 0.1 * jax.random.normal(splits[7], (D,), jnp.float32), 0.5, 1.5)
    kernel = scatter_about(splits[8], (KW, D), KW ** -0.5, 1.0, (), jnp.float32)
    w_in = scatter_about(splits[9], (D, 2 * D), D ** -0.5, 0.15625, ((0, 8),))
    w_conv_out = scatter_about(splits[10], (D, D), D ** -0.5, 0.15625, ((0, 8),))
    w_attn_out = scatter_about(splits[11], (D, D), D ** -0.5, 0.15625, ((0, 8),))
    return dict(grad_out=grad_out, saved_input=saved_input, pre_glu=pre_glu, queries=queries, keys=keys, values=values, frame_counts=frame_counts, norm_gain=norm_gain, kernel=kernel, w_in=w_in, w_conv_out=w_conv_out, w_attn_out=w_attn_out)


def segments_of(frame_lens, positions):
    ends = jnp.cumsum(frame_lens).astype(jnp.int32)
    counted = lax.optimization_barrier(jnp.sum((positions[:, None] >= ends[None, :]).astype(jnp.int32), axis=1)).astype(jnp.int32)
    return jnp.where(positions < 0, jnp.int32(-1), counted).astype(jnp.int32)

def group_conv(grad_rows, input_rows, pre_rows, frame_lens, norm_gain, kernel, w_in, w_conv_out, w_attn_out):
    half = KW // 2
    length = grad_rows.shape[0]
    seg_own = segments_of(frame_lens, jnp.arange(length, dtype=jnp.int32))
    seg_pad = segments_of(frame_lens, jnp.arange(-half, length + half, dtype=jnp.int32))
    first_half = pre_rows[:, :D].astype(jnp.float32)
    gate_sig = jax.nn.sigmoid(pre_rows[:, D:].astype(jnp.float32))
    glu_out = (first_half * gate_sig).astype(jnp.bfloat16)
    glu_pad = jnp.pad(glu_out.astype(jnp.float32), ((half, half), (0, 0)))
    conv_out = jnp.zeros((length, D), jnp.float32)
    for tap_index in range(KW):
        match = (seg_pad[tap_index:tap_index + length] == seg_own).astype(jnp.float32)[:, None]
        conv_out = conv_out + kernel[tap_index] * glu_pad[tap_index:tap_index + length] * match
    conv_out_grad = jnp.dot(grad_rows, w_conv_out.T, preferred_element_type=jnp.float32)
    conv_sig = jax.nn.sigmoid(conv_out)
    conv_grad = (conv_out_grad * conv_sig * (1.0 + conv_out * (1.0 - conv_sig))).astype(jnp.bfloat16)
    grad_float = conv_grad.astype(jnp.float32)
    grad_pad = jnp.pad(grad_float, ((half, half), (0, 0)))
    glu_grad = jnp.zeros((length, D), jnp.float32)
    kernel_rows = []
    for tap_index in range(KW):
        back = 2 * half - tap_index
        match_back = (seg_pad[back:back + length] == seg_own).astype(jnp.float32)[:, None]
        glu_grad = glu_grad + kernel[tap_index] * grad_pad[back:back + length] * match_back
        match = (seg_pad[tap_index:tap_index + length] == seg_own).astype(jnp.float32)[:, None]
        kernel_rows.append(lax.optimization_barrier(jnp.sum(grad_float * glu_pad[tap_index:tap_index + length] * match, axis=0)))
    glu_in_grad = jnp.concatenate([glu_grad * gate_sig, glu_grad * first_half * gate_sig * (1.0 - gate_sig)], axis=1).astype(jnp.bfloat16)
    norm_grad = jnp.dot(glu_in_grad, w_in.T, preferred_element_type=jnp.float32)
    inputs = input_rows.astype(jnp.float32)
    centred = inputs - lax.optimization_barrier(jnp.mean(inputs, axis=1, keepdims=True))
    inv_std = 1.0 / jnp.sqrt(lax.optimization_barrier(jnp.mean(centred * centred, axis=1, keepdims=True)) + 1e-05)
    normed = centred * inv_std
    scaled_grad = norm_grad * norm_gain
    input_grad = inv_std * (scaled_grad - lax.optimization_barrier(jnp.mean(scaled_grad, axis=1, keepdims=True)) - normed * lax.optimization_barrier(jnp.mean(scaled_grad * normed, axis=1, keepdims=True)))
    resid_grad = (grad_rows.astype(jnp.float32) + input_grad).astype(jnp.bfloat16)
    gain_term = lax.optimization_barrier(jnp.sum(norm_grad * normed, axis=0))
    ctx_grad = jnp.dot(resid_grad, w_attn_out.T, preferred_element_type=jnp.float32).astype(jnp.bfloat16)
    return (resid_grad, ctx_grad, jnp.stack(kernel_rows), gain_term, seg_own)

def head_backward(query_head, key_head, value_head, out_grad, seg_own):
    scale = 1.0 / math.sqrt(HD)
    scores = jnp.dot(query_head, key_head.T, preferred_element_type=jnp.float32) * scale
    scores = jnp.where(seg_own[:, None] == seg_own[None, :], scores, -1e+30)
    peak = lax.optimization_barrier(jnp.max(scores, axis=1, keepdims=True))
    expd = jnp.exp(scores - peak)
    probs = expd / lax.optimization_barrier(jnp.sum(expd, axis=1, keepdims=True))
    probs_low = probs.astype(jnp.bfloat16)
    value_grad = jnp.dot(probs_low.T, out_grad, preferred_element_type=jnp.float32).astype(jnp.bfloat16)
    prob_grad = jnp.dot(out_grad, value_head.T, preferred_element_type=jnp.float32)
    delta = lax.optimization_barrier(jnp.sum(probs * prob_grad, axis=1, keepdims=True))
    score_grad = (probs * (prob_grad - delta)).astype(jnp.bfloat16)
    query_grad = (jnp.dot(score_grad, key_head, preferred_element_type=jnp.float32) * scale).astype(jnp.bfloat16)
    key_grad = (jnp.dot(score_grad.T, query_head, preferred_element_type=jnp.float32) * scale).astype(jnp.bfloat16)
    return (query_grad, key_grad, value_grad)

def reference(grad_out, saved_input, pre_glu, queries, keys, values, frame_counts, norm_gain, kernel, w_in, w_conv_out, w_attn_out):

    def split_heads(array):
        return array.reshape(TOTAL, H, HD).transpose(1, 0, 2)

    def join_heads(array):
        return array.transpose(1, 0, 2).reshape(TOTAL, D)

    def one_group(items):
        grad_rows, input_rows, pre_rows, query_rows, key_rows, value_rows, frame_lens = items
        resid_grad, ctx_grad, kernel_term, gain_term, seg_own = group_conv(grad_rows, input_rows, pre_rows, frame_lens, norm_gain, kernel, w_in, w_conv_out, w_attn_out)
        query_grad, key_grad, value_grad = lax.map(lambda heads: head_backward(heads[0], heads[1], heads[2], heads[3], seg_own), (split_heads(query_rows), split_heads(key_rows), split_heads(value_rows), split_heads(ctx_grad)))
        return (resid_grad, join_heads(query_grad), join_heads(key_grad), join_heads(value_grad), kernel_term, gain_term)
    groups = (grad_out.reshape(N_DP, TOTAL, D), saved_input.reshape(N_DP, TOTAL, D), pre_glu.reshape(N_DP, TOTAL, 2 * D), queries.reshape(N_DP, TOTAL, D), keys.reshape(N_DP, TOTAL, D), values.reshape(N_DP, TOTAL, D), frame_counts)
    resid_grad, query_grad, key_grad, value_grad, kernel_terms, gain_terms = lax.map(one_group, groups)
    return (resid_grad.reshape(FRAMES, D), query_grad.reshape(FRAMES, D), key_grad.reshape(FRAMES, D), value_grad.reshape(FRAMES, D), lax.optimization_barrier(jnp.sum(kernel_terms, axis=0)), lax.optimization_barrier(jnp.sum(gain_terms, axis=0)))
```

```python
import math

import jax
import jax.numpy as jnp
from jax import lax
from jax.experimental import pallas as pl
from jax.experimental.pallas import tpu as pltpu
from jax.sharding import PartitionSpec as P

HD = 80
KW = 31


def padded(block, sides, width):
    for axis, dim in sides:
        count = lax.axis_size(axis)
        forward = [(i, i + 1) for i in range(count - 1)]
        backward = [(target, source) for source, target in forward]
        low = lax.ppermute(
            lax.slice_in_dim(block, block.shape[dim] - width, None, axis=dim), axis, forward
        )
        high = lax.ppermute(lax.slice_in_dim(block, 0, width, axis=dim), axis, backward)
        block = jnp.concatenate([low, block, high], axis=dim)
    return block


def segments_of(frame_lens, positions):
    ends = jnp.cumsum(frame_lens)
    counted = jnp.sum((positions[:, None] >= ends[None, :]).astype(jnp.int32), axis=1)
    return jnp.where(positions < 0, jnp.int32(-1), counted)


def row_product(active, piece):
    return jnp.einsum("tc,rc->tr", active, piece, preferred_element_type=jnp.float32)


def attention_backward(query_rows, key_rows, value_rows, out_grad, seg_all):
    total, columns = query_rows.shape
    heads = columns // HD
    scale = 1.0 / math.sqrt(HD)
    query_heads = query_rows.reshape(total, heads, HD)
    key_heads = key_rows.reshape(total, heads, HD)
    value_heads = value_rows.reshape(total, heads, HD)
    grad_heads = out_grad.reshape(total, heads, HD)
    qblock = min(512, total)
    nblocks = total // qblock

    def block_step(block, carry):
        query_out, key_acc, value_acc = carry
        qstart = block * qblock
        query_block = lax.dynamic_slice_in_dim(query_heads, qstart, qblock, 0)
        grad_block = lax.dynamic_slice_in_dim(grad_heads, qstart, qblock, 0)
        seg_query = lax.dynamic_slice_in_dim(seg_all, qstart, qblock, 0)
        scores = (
            jnp.einsum("qhd,khd->hqk", query_block, key_heads, preferred_element_type=jnp.float32)
            * scale
        )
        scores = jnp.where((seg_query[:, None] == seg_all[None, :])[None], scores, -1e30)
        peak = jnp.max(scores, axis=2, keepdims=True)
        expd = jnp.exp(scores - peak)
        probs = expd / jnp.sum(expd, axis=2, keepdims=True)
        probs_low = probs.astype(jnp.bfloat16)
        value_part = jnp.einsum(
            "hqk,qhd->khd", probs_low, grad_block, preferred_element_type=jnp.float32
        )
        prob_grad = jnp.einsum(
            "qhd,khd->hqk", grad_block, value_heads, preferred_element_type=jnp.float32
        )
        delta = jnp.sum(probs * prob_grad, axis=2, keepdims=True)
        score_grad = (probs * (prob_grad - delta)).astype(jnp.bfloat16)
        query_part = (
            jnp.einsum("hqk,khd->qhd", score_grad, key_heads, preferred_element_type=jnp.float32)
            * scale
        ).astype(jnp.bfloat16)
        key_part = jnp.einsum(
            "hqk,qhd->khd", score_grad, query_block, preferred_element_type=jnp.float32
        )
        query_out = lax.dynamic_update_slice_in_dim(query_out, query_part, qstart, 0)
        return (query_out, key_acc + key_part, value_acc + value_part)

    initial = (
        jnp.zeros((total, heads, HD), jnp.bfloat16),
        jnp.zeros((total, heads, HD), jnp.float32),
        jnp.zeros((total, heads, HD), jnp.float32),
    )
    query_out, key_acc, value_acc = lax.fori_loop(0, nblocks, block_step, initial)
    key_grad = (key_acc * scale).astype(jnp.bfloat16)
    value_grad = value_acc.astype(jnp.bfloat16)
    return (
        query_out.reshape(total, columns),
        key_grad.reshape(total, columns),
        value_grad.reshape(total, columns),
    )


def local(
    grad_out,
    saved_input,
    pre_glu,
    queries,
    keys,
    values,
    frame_counts,
    norm_gain,
    kernel,
    w_in,
    w_conv_out,
    w_attn_out,
):
    t_dev, width = grad_out.shape
    n_seq = lax.axis_size("seq")
    total = t_dev * n_seq
    half = KW // 2
    frame_lens = frame_counts[0]
    seq_index = lax.axis_index("seq")
    ext_pos = seq_index * t_dev + jnp.arange(-half, t_dev + half, dtype=jnp.int32)
    seg_ext = segments_of(frame_lens, ext_pos)
    seg_own = seg_ext[half : half + t_dev]
    first_half = pre_glu[:, :width].astype(jnp.float32)
    gate_sig = jax.nn.sigmoid(pre_glu[:, width:].astype(jnp.float32))
    glu_out = (first_half * gate_sig).astype(jnp.bfloat16)
    glu_ext = padded(glu_out, (("seq", 0),), half).astype(jnp.float32)
    matches = [
        (seg_ext[tap_index : tap_index + t_dev] == seg_own).astype(jnp.float32)[:, None]
        for tap_index in range(KW)
    ]
    conv_out = jnp.zeros((t_dev, width), jnp.float32)
    for tap_index in range(KW):
        conv_out = (
            conv_out
            + kernel[tap_index] * glu_ext[tap_index : tap_index + t_dev] * matches[tap_index]
        )
    conv_out_grad = row_product(grad_out, lax.all_gather(w_conv_out, "dp", axis=0, tiled=True))
    conv_sig = jax.nn.sigmoid(conv_out)
    conv_grad = (conv_out_grad * conv_sig * (1.0 + conv_out * (1.0 - conv_sig))).astype(
        jnp.bfloat16
    )
    grad_ext = padded(conv_grad, (("seq", 0),), half).astype(jnp.float32)
    grad_float = grad_ext[half : half + t_dev]
    glu_grad = jnp.zeros((t_dev, width), jnp.float32)
    kernel_rows = []
    for tap_index in range(KW):
        back = 2 * half - tap_index
        glu_grad = glu_grad + kernel[tap_index] * grad_ext[back : back + t_dev] * matches[back]
        kernel_rows.append(
            jnp.sum(
                grad_float * glu_ext[tap_index : tap_index + t_dev] * matches[tap_index], axis=0
            )
        )
    glu_in_grad = jnp.concatenate(
        [glu_grad * gate_sig, glu_grad * first_half * gate_sig * (1.0 - gate_sig)], axis=1
    ).astype(jnp.bfloat16)
    norm_grad = row_product(glu_in_grad, lax.all_gather(w_in, "dp", axis=0, tiled=True))
    inputs = saved_input.astype(jnp.float32)
    centred = inputs - jnp.mean(inputs, axis=1, keepdims=True)
    inv_std = 1.0 / jnp.sqrt(jnp.mean(centred * centred, axis=1, keepdims=True) + 1e-05)
    normed = centred * inv_std
    scaled_grad = norm_grad * norm_gain
    input_grad = inv_std * (
        scaled_grad
        - jnp.mean(scaled_grad, axis=1, keepdims=True)
        - normed * jnp.mean(scaled_grad * normed, axis=1, keepdims=True)
    )
    resid_grad = (grad_out.astype(jnp.float32) + input_grad).astype(jnp.bfloat16)
    gain_term = jnp.sum(norm_grad * normed, axis=0)
    ctx_float = row_product(resid_grad, lax.all_gather(w_attn_out, "dp", axis=0, tiled=True))
    ctx_grad = ctx_float.astype(jnp.bfloat16)
    relayed = lax.all_to_all(ctx_grad, "seq", split_axis=1, concat_axis=0, tiled=True)
    seg_all = segments_of(frame_lens, jnp.arange(total, dtype=jnp.int32))
    query_grad, key_grad, value_grad = attention_backward(queries, keys, values, relayed, seg_all)
    kernel_grad, gain_grad = lax.psum((jnp.stack(kernel_rows), gain_term), ("dp", "seq"))
    return (resid_grad, query_grad, key_grad, value_grad, kernel_grad, gain_grad)


MESH = pl.DeviceIdType.MESH
NT = (((1,), (1,)), ((), ()))
NN = (((1,), (0,)), ((), ()))
TN = (((0,), (0,)), ((), ()))
PART = 48
LANES = 128
COPIES = 59


def fused(
    go_ref, x_ref, pre_ref, q_ref, k_ref, v_ref, counts_ref, gain_ref, kern_ref,
    w_in_ref, w_conv_ref, w_attn_ref,
    resid_ref, qg_ref, kg_ref, vg_ref, taps_ref, gaing_ref,
    full_conv, full_in, full_attn, glu_ref, gext_ref, halo_ref, seg_ref, segc_ref,
    conv_ref, cog_ref, cg_ref, cext_ref, gin_ref, ng_ref, probs_ref, ctx_ref, dout_ref,
    qa_ref, ka_ref, va_ref, sums_ref, part_a, mine_a, part_b, total_ref,
    send_sem, recv_sem, local_sem,
):
    f32, bf16 = jnp.float32, jnp.bfloat16
    rows, width = go_ref.shape
    total, cols = q_ref.shape
    heads = cols // HD
    n_seq = total // rows
    n_dp = 8
    shard = width // n_dp
    half = KW // 2
    me, z = lax.axis_index("dp"), lax.axis_index("seq")
    core = me % 2
    sib = me + 1 - 2 * core
    xn = me + 2 - 4 * ((me // 2) % 2)
    yn = me + 4 - 8 * (me // 4)
    diag = xn + 4 - 8 * (me // 4)
    over = 1 - 2 * core
    zn = z + 1 - 2 * (z % 2)
    moff = PART * (z % 2)
    toff = PART - moff

    barrier = pltpu.get_barrier_semaphore()
    for s in range(1, n_dp):
        pl.semaphore_signal(barrier, inc=1, device_id=((me + s) % n_dp, z), device_id_type=MESH)
    for s in range(1, n_seq):
        pl.semaphore_signal(barrier, inc=1, device_id=(me, (z + s) % n_seq), device_id_type=MESH)
    pl.semaphore_wait(barrier, n_dp + n_seq - 2)

    sent = []

    def remote(src, dst, idx, dp, seq):
        return pltpu.make_async_remote_copy(
            src_ref=src, dst_ref=dst, send_sem=send_sem.at[idx], recv_sem=recv_sem.at[idx],
            device_id=(dp, seq), device_id_type=MESH,
        )

    def push(src, dst, idx, dp, seq):
        copy = remote(src, dst, idx, dp, seq)
        copy.start()
        sent.append(copy)

    def arrive(dst, idx):
        remote(dst, dst, idx, sib, z).wait_recv()

    weights = ((w_conv_ref, full_conv), (w_in_ref, full_in), (w_attn_ref, full_attn))

    def span(start, size):
        return pl.ds(pl.multiple_of(start, 16), size)

    def piece(m, owner, off, size):
        return weights[m][1].at[span(owner * shard + off, size), :]

    rest = shard - 2 * PART
    own_copies = [
        pltpu.make_async_copy(weights[m][0], piece(m, me, 0, shard), local_sem.at[m])
        for m in range(3)
    ]

    def send_own(m):
        base = 13 * m
        source = weights[m][0]
        for k, dev in ((0, xn), (2, yn)):
            push(source.at[span(moff, PART), :], piece(m, me, moff, PART), base + k, dev, z)
            push(source.at[pl.ds(2 * PART, rest), :], piece(m, me, 2 * PART, rest), base + k + 1, dev, z)
        push(source, piece(m, me, 0, shard), base + 9, sib, z)
        own_copies[m].start()

    def forward_xy(m):
        base = 13 * m
        for k, dev in ((0, xn), (2, yn)):
            arrive(piece(m, dev, moff, PART), base + k)
            arrive(piece(m, dev, 2 * PART, rest), base + k + 1)
        via = core * yn + (1 - core) * xn
        owner = core * xn + (1 - core) * yn
        for k, off, size in ((4, moff, PART), (5, 2 * PART, rest)):
            push(piece(m, owner, off, size), piece(m, owner, off, size), base + k, via, z)
        for k, dev in ((6, xn), (7, yn)):
            push(piece(m, dev, moff, PART), piece(m, dev, moff, PART), base + k, me, zn)

    def forward_diag(m):
        base = 13 * m
        arrive(piece(m, diag, moff, PART), base + 4)
        push(piece(m, diag, moff, PART), piece(m, diag, moff, PART), base + 8, me, zn)
        arrive(piece(m, diag, 2 * PART, rest), base + 5)
        for k, dev in ((6, xn), (7, yn)):
            arrive(piece(m, dev, toff, PART), base + k)
            push(piece(m, dev, 0, shard), piece(m, dev, 0, shard), base + k + 4, sib, z)

    def finish(m):
        base = 13 * m
        arrive(piece(m, diag, toff, PART), base + 8)
        push(piece(m, diag, 0, shard), piece(m, diag, 0, shard), base + 12, sib, z)
        for k, dev in ((9, sib), (10, xn + over), (11, yn + over), (12, diag + over)):
            arrive(piece(m, dev, 0, shard), base + k)
        own_copies[m].wait()

    def segments(pos):
        end = jnp.int32(0)
        seg = jnp.zeros(pos.shape, jnp.int32)
        for u in range(counts_ref.shape[1]):
            end = end + counts_ref[0, u]
            seg = seg + jnp.where(pos >= end, 1, 0)
        return jnp.where(pos < 0, -1, seg)

    def tiles(n, size):
        return pl.ds(pl.multiple_of(n * size, size), size)

    prev, following = (z + n_seq - 1) % n_seq, (z + 1) % n_seq

    def send_halo(src, slot, idx):
        push(src.at[pl.ds(rows - 16, 16), :], halo_ref.at[slot], idx, me, following)
        push(src.at[pl.ds(0, 16), :], halo_ref.at[slot + 1], idx + 1, me, prev)

    def take_halo(dst, slot, idx):
        arrive(halo_ref.at[slot], idx)
        arrive(halo_ref.at[slot + 1], idx + 1)
        dst[0:16, :] = halo_ref[slot].astype(f32)
        dst[rows + 16 : rows + 32, :] = halo_ref[slot + 1].astype(f32)

    send_own(0)

    @pl.loop(0, width // LANES)
    def _(n):
        c = tiles(n, LANES)
        c2 = pl.ds(pl.multiple_of(width + n * LANES, LANES), LANES)
        gate = jax.nn.sigmoid(pre_ref[:, c2].astype(f32))
        glu = (pre_ref[:, c].astype(f32) * gate).astype(bf16)
        glu_ref[:, c] = glu
        gext_ref[16 : 16 + rows, c] = glu.astype(f32)

    send_halo(glu_ref, 0, 39)

    seg_ref[...] = segments(
        z * rows - 16 + lax.broadcasted_iota(jnp.int32, (rows + 32, LANES), 0)
    )
    segc_ref[...] = segments(lax.broadcasted_iota(jnp.int32, (total, LANES), 0))

    scale = 1.0 / math.sqrt(HD)
    qblock = 256

    def window(h):
        low = h * HD // LANES * LANES
        high = min(-(-(h + 1) * HD // LANES) * LANES, cols)
        lane = low + lax.broadcasted_iota(jnp.int32, (1, high - low), 1)
        inside = jnp.where((lane >= h * HD) & (lane < (h + 1) * HD), 1.0, 0.0).astype(bf16)
        return low, high, inside

    def make_probs(h):
        low, high, inside = window(h)

        @pl.loop(0, total // qblock)
        def _(b):
            queries = q_ref[tiles(b, qblock), low:high]
            scores = (
                lax.dot_general(k_ref[:, low:high] * inside, queries, NT, preferred_element_type=f32)
                * scale
            )
            seg_q = segments(b * qblock + lax.broadcasted_iota(jnp.int32, (1, qblock), 1))
            seg_k = jnp.concatenate([segc_ref[...]] * (qblock // LANES), axis=1)
            scores = jnp.where(seg_k == seg_q, scores, -1e30)
            expd = jnp.exp(scores - jnp.max(scores, axis=0, keepdims=True))
            probs_ref[h, b] = expd * (1.0 / jnp.sum(expd, axis=0, keepdims=True))

    make_probs(0)
    forward_xy(0)
    send_own(1)

    take_halo(gext_ref, 0, 39)

    @pl.loop(0, width // LANES)
    def _(n):
        c = tiles(n, LANES)
        seg_own = seg_ref[16 : 16 + rows, :]
        acc = jnp.zeros((rows, LANES), f32)
        for o in range(KW):
            same = seg_ref[o + 1 : o + 1 + rows, :] == seg_own
            acc = acc + kern_ref[o : o + 1, c] * jnp.where(
                same, gext_ref[o + 1 : o + 1 + rows, c], 0.0
            )
        conv_ref[:, c] = acc

    forward_diag(0)
    for h in range(1, heads):
        make_probs(h)
    finish(0)

    @pl.loop(0, width // 256)
    def _(n):
        c = tiles(n, 256)
        cog_ref[:, c] = lax.dot_general(go_ref[...], full_conv[c, :], NT, preferred_element_type=f32)

    @pl.loop(0, width // LANES)
    def _(n):
        c = tiles(n, LANES)
        conv = conv_ref[:, c]
        sig = jax.nn.sigmoid(conv)
        grad = (cog_ref[:, c] * sig * (1.0 + conv * (1.0 - sig))).astype(bf16)
        cg_ref[:, c] = grad
        cext_ref[16 : 16 + rows, c] = grad.astype(f32)

    send_halo(cg_ref, 2, 41)
    forward_xy(1)
    send_own(2)
    take_halo(cext_ref, 2, 41)

    @pl.loop(0, width // LANES)
    def _(n):
        c = tiles(n, LANES)
        c2 = pl.ds(pl.multiple_of(width + n * LANES, LANES), LANES)
        seg_own = seg_ref[16 : 16 + rows, :]
        grad_own = cext_ref[16 : 16 + rows, c]
        acc = jnp.zeros((rows, LANES), f32)
        for o in range(KW):
            same = seg_ref[o + 1 : o + 1 + rows, :] == seg_own
            near = jnp.where(same, cext_ref[o + 1 : o + 1 + rows, c], 0.0)
            acc = acc + kern_ref[KW - 1 - o : KW - o, c] * near
            pair = jnp.where(same, grad_own * gext_ref[o + 1 : o + 1 + rows, c], 0.0)
            sums_ref[o : o + 1, c] = jnp.sum(pair, axis=0, keepdims=True)
        gate = jax.nn.sigmoid(pre_ref[:, c2].astype(f32))
        scaled = acc * gate
        gin_ref[:, c] = scaled.astype(bf16)
        gin_ref[:, c2] = (scaled * pre_ref[:, c].astype(f32) * (1.0 - gate)).astype(bf16)

    forward_diag(1)
    finish(1)

    @pl.loop(0, width // 256)
    def _(n):
        c = tiles(n, 256)
        ng_ref[:, c] = lax.dot_general(gin_ref[...], full_in[c, :], NT, preferred_element_type=f32)

    forward_xy(2)
    sums_ref[KW : KW + 1, :] = jnp.zeros((1, width), f32)

    @pl.loop(0, rows // 16)
    def _(n):
        r = tiles(n, 16)
        x = x_ref[r, :].astype(f32)
        centred = x - jnp.mean(x, axis=1, keepdims=True)
        inv = 1.0 / jnp.sqrt(jnp.mean(centred * centred, axis=1, keepdims=True) + 1e-05)
        normed = centred * inv
        grad = ng_ref[r, :]
        scaled = grad * gain_ref[...]
        back = inv * (
            scaled
            - jnp.mean(scaled, axis=1, keepdims=True)
            - normed * jnp.mean(scaled * normed, axis=1, keepdims=True)
        )
        resid_ref[r, :] = (go_ref[r, :].astype(f32) + back).astype(bf16)
        sums_ref[KW : KW + 1, :] += jnp.sum(grad * normed, axis=0, keepdims=True)

    forward_diag(2)
    for s in range(1, n_seq):
        to = (z + s) % n_seq
        push(sums_ref.at[tiles(to, 8), :], part_a.at[s - 1], 45 + s, me, to)
    finish(2)

    for s in range(1, n_seq + 1):
        to = (z + s) % n_seq
        out = lax.dot_general(
            resid_ref[...], full_attn[tiles(to, cols), :], NT, preferred_element_type=f32
        ).astype(bf16)
        if s < n_seq:
            ctx_ref[s - 1] = out
            push(ctx_ref.at[s - 1], dout_ref.at[tiles(z, rows), :], 42 + s, me, to)
        else:
            dout_ref[tiles(z, rows), :] = out

    for s in range(1, n_seq):
        arrive(part_a.at[s - 1], 45 + s)
    mine_a[...] = sums_ref[tiles(z, 8), :] + part_a[0] + part_a[1] + part_a[2]
    for s in range(1, n_dp):
        push(mine_a, part_b.at[me], 48 + s, (me + s) % n_dp, z)
    part_b[me] = mine_a[...]

    for s in range(1, n_seq):
        arrive(dout_ref.at[tiles((z + n_seq - s) % n_seq, rows), :], 42 + s)

    qa_ref[...] = jnp.zeros((total, cols), f32)
    ka_ref[...] = jnp.zeros((total, cols), f32)
    va_ref[...] = jnp.zeros((total, cols), f32)
    for h in range(heads):
        low, high, inside = window(h)

        @pl.loop(0, total // qblock)
        def _(b):
            r = tiles(b, qblock)
            probs = probs_ref[h, b]
            dout = dout_ref[r, low:high] * inside
            va_ref[:, low:high] += lax.dot_general(
                probs.astype(bf16), dout, NN, preferred_element_type=f32
            )
            prob_grad = lax.dot_general(v_ref[:, low:high], dout, NT, preferred_element_type=f32)
            delta = jnp.sum(probs * prob_grad, axis=0, keepdims=True)
            score_grad = (probs * (prob_grad - delta)).astype(bf16)
            ka_ref[:, low:high] += lax.dot_general(
                score_grad, q_ref[r, low:high] * inside, NN, preferred_element_type=f32
            )
            qa_ref[r, low:high] += lax.dot_general(
                score_grad, k_ref[:, low:high] * inside, TN, preferred_element_type=f32
            )

        if h == 1:
            for s in range(1, n_dp):
                arrive(part_b.at[(me + n_dp - s) % n_dp], 48 + s)
            chunk = part_b[0]
            for i in range(1, n_dp):
                chunk = chunk + part_b[i]
            total_ref[tiles(z, 8), :] = chunk
            for s in range(1, n_seq):
                block = total_ref.at[tiles(z, 8), :]
                push(block, block, 55 + s, me, (z + s) % n_seq)

    qg_ref[...] = (qa_ref[...] * scale).astype(bf16)
    kg_ref[...] = (ka_ref[...] * scale).astype(bf16)
    vg_ref[...] = va_ref[...].astype(bf16)
    for s in range(1, n_seq):
        arrive(total_ref.at[tiles((z + n_seq - s) % n_seq, 8), :], 55 + s)
    taps_ref[...] = total_ref[0:KW, :]
    gaing_ref[...] = total_ref[KW : KW + 1, :]
    for copy in sent:
        copy.wait_send()


def fused_local(
    grad_out, saved_input, pre_glu, queries, keys, values, frame_counts, norm_gain, kernel,
    w_in, w_conv_out, w_attn_out,
):
    rows, width = grad_out.shape
    total, cols = queries.shape
    heads = cols // HD
    f32, bf16 = jnp.float32, jnp.bfloat16
    vmem = pl.BlockSpec(memory_space=pltpu.VMEM)
    smem = pl.BlockSpec(memory_space=pltpu.SMEM)
    hbm = pl.BlockSpec(memory_space=pl.ANY)
    outs = pl.pallas_call(
        fused,
        out_shape=(
            jax.ShapeDtypeStruct((rows, width), bf16),
            jax.ShapeDtypeStruct((total, cols), bf16),
            jax.ShapeDtypeStruct((total, cols), bf16),
            jax.ShapeDtypeStruct((total, cols), bf16),
            jax.ShapeDtypeStruct((KW, width), f32),
            jax.ShapeDtypeStruct((1, width), f32),
        ),
        in_specs=[vmem] * 6 + [smem] + [vmem] * 2 + [hbm] * 3,
        out_specs=(vmem,) * 6,
        scratch_shapes=[
            pltpu.VMEM((width, width), bf16),
            pltpu.VMEM((width, 2 * width), bf16),
            pltpu.VMEM((width, width), bf16),
            pltpu.VMEM((rows, width), bf16),
            pltpu.VMEM((rows + 32, width), f32),
            pltpu.VMEM((4, 16, width), bf16),
            pltpu.VMEM((rows + 32, LANES), jnp.int32),
            pltpu.VMEM((total, LANES), jnp.int32),
            pltpu.VMEM((rows, width), f32),
            pltpu.VMEM((rows, width), f32),
            pltpu.VMEM((rows, width), bf16),
            pltpu.VMEM((rows + 32, width), f32),
            pltpu.VMEM((rows, 2 * width), bf16),
            pltpu.VMEM((rows, width), f32),
            pltpu.VMEM((heads, total // 256, total, 256), f32),
            pltpu.VMEM((3, rows, cols), bf16),
            pltpu.VMEM((total, cols), bf16),
            pltpu.VMEM((total, cols), f32),
            pltpu.VMEM((total, cols), f32),
            pltpu.VMEM((total, cols), f32),
            pltpu.VMEM((KW + 1, width), f32),
            pltpu.VMEM((3, 8, width), f32),
            pltpu.VMEM((8, width), f32),
            pltpu.VMEM((8, 8, width), f32),
            pltpu.VMEM((KW + 1, width), f32),
            pltpu.SemaphoreType.DMA((COPIES,)),
            pltpu.SemaphoreType.DMA((COPIES,)),
            pltpu.SemaphoreType.DMA((3,)),
        ],
        compiler_params=pltpu.CompilerParams(
            collective_id=0, has_side_effects=True, vmem_limit_bytes=50 * 1024 * 1024
        ),
    )(
        grad_out, saved_input, pre_glu, queries, keys, values, frame_counts,
        norm_gain.reshape(1, width), kernel, w_in, w_conv_out, w_attn_out,
    )
    return outs[:5] + (outs[5].reshape(width),)


def solution(mesh):
    in_specs = (
        P(("dp", "seq"), None),
        P(("dp", "seq"), None),
        P(("dp", "seq"), None),
        P("dp", "seq"),
        P("dp", "seq"),
        P("dp", "seq"),
        P("dp", None),
        P(),
        P(),
        P("dp", None),
        P("dp", None),
        P("dp", None),
    )
    out_specs = (P(("dp", "seq"), None), P("dp", "seq"), P("dp", "seq"), P("dp", "seq"), P(), P())
    small = mesh.shape["dp"] == 8 and mesh.shape["seq"] == 4
    body = fused_local if small else local
    return jax.shard_map(body, mesh=mesh, in_specs=in_specs, out_specs=out_specs, check_vma=False)
```

```python
import math

import jax
import jax.numpy as jnp
from jax import lax
from jax.experimental import pallas as pl
from jax.experimental.pallas import tpu as pltpu
from jax.sharding import PartitionSpec as P

HD = 80
KW = 31


def padded(block, sides, width):
    for axis, dim in sides:
        count = lax.axis_size(axis)
        forward = [(i, i + 1) for i in range(count - 1)]
        backward = [(target, source) for source, target in forward]
        low = lax.ppermute(
            lax.slice_in_dim(block, block.shape[dim] - width, None, axis=dim), axis, forward
        )
        high = lax.ppermute(lax.slice_in_dim(block, 0, width, axis=dim), axis, backward)
        block = jnp.concatenate([low, block, high], axis=dim)
    return block


def segments_of(frame_lens, positions):
    ends = jnp.cumsum(frame_lens)
    counted = jnp.sum((positions[:, None] >= ends[None, :]).astype(jnp.int32), axis=1)
    return jnp.where(positions < 0, jnp.int32(-1), counted)


def row_product(active, piece):
    return jnp.einsum("tc,rc->tr", active, piece, preferred_element_type=jnp.float32)


def attention_backward(query_rows, key_rows, value_rows, out_grad, seg_all):
    total, columns = query_rows.shape
    heads = columns // HD
    scale = 1.0 / math.sqrt(HD)
    query_heads = query_rows.reshape(total, heads, HD)
    key_heads = key_rows.reshape(total, heads, HD)
    value_heads = value_rows.reshape(total, heads, HD)
    grad_heads = out_grad.reshape(total, heads, HD)
    qblock = min(512, total)
    nblocks = total // qblock

    def block_step(block, carry):
        query_out, key_acc, value_acc = carry
        qstart = block * qblock
        query_block = lax.dynamic_slice_in_dim(query_heads, qstart, qblock, 0)
        grad_block = lax.dynamic_slice_in_dim(grad_heads, qstart, qblock, 0)
        seg_query = lax.dynamic_slice_in_dim(seg_all, qstart, qblock, 0)
        scores = (
            jnp.einsum("qhd,khd->hqk", query_block, key_heads, preferred_element_type=jnp.float32)
            * scale
        )
        scores = jnp.where((seg_query[:, None] == seg_all[None, :])[None], scores, -1e30)
        peak = jnp.max(scores, axis=2, keepdims=True)
        expd = jnp.exp(scores - peak)
        probs = expd / jnp.sum(expd, axis=2, keepdims=True)
        probs_low = probs.astype(jnp.bfloat16)
        value_part = jnp.einsum(
            "hqk,qhd->khd", probs_low, grad_block, preferred_element_type=jnp.float32
        )
        prob_grad = jnp.einsum(
            "qhd,khd->hqk", grad_block, value_heads, preferred_element_type=jnp.float32
        )
        delta = jnp.sum(probs * prob_grad, axis=2, keepdims=True)
        score_grad = (probs * (prob_grad - delta)).astype(jnp.bfloat16)
        query_part = (
            jnp.einsum("hqk,khd->qhd", score_grad, key_heads, preferred_element_type=jnp.float32)
            * scale
        ).astype(jnp.bfloat16)
        key_part = jnp.einsum(
            "hqk,qhd->khd", score_grad, query_block, preferred_element_type=jnp.float32
        )
        query_out = lax.dynamic_update_slice_in_dim(query_out, query_part, qstart, 0)
        return (query_out, key_acc + key_part, value_acc + value_part)

    initial = (
        jnp.zeros((total, heads, HD), jnp.bfloat16),
        jnp.zeros((total, heads, HD), jnp.float32),
        jnp.zeros((total, heads, HD), jnp.float32),
    )
    query_out, key_acc, value_acc = lax.fori_loop(0, nblocks, block_step, initial)
    key_grad = (key_acc * scale).astype(jnp.bfloat16)
    value_grad = value_acc.astype(jnp.bfloat16)
    return (
        query_out.reshape(total, columns),
        key_grad.reshape(total, columns),
        value_grad.reshape(total, columns),
    )


def local(
    grad_out,
    saved_input,
    pre_glu,
    queries,
    keys,
    values,
    frame_counts,
    norm_gain,
    kernel,
    w_in,
    w_conv_out,
    w_attn_out,
):
    t_dev, width = grad_out.shape
    n_seq = lax.axis_size("seq")
    total = t_dev * n_seq
    half = KW // 2
    frame_lens = frame_counts[0]
    seq_index = lax.axis_index("seq")
    ext_pos = seq_index * t_dev + jnp.arange(-half, t_dev + half, dtype=jnp.int32)
    seg_ext = segments_of(frame_lens, ext_pos)
    seg_own = seg_ext[half : half + t_dev]
    first_half = pre_glu[:, :width].astype(jnp.float32)
    gate_sig = jax.nn.sigmoid(pre_glu[:, width:].astype(jnp.float32))
    glu_out = (first_half * gate_sig).astype(jnp.bfloat16)
    glu_ext = padded(glu_out, (("seq", 0),), half).astype(jnp.float32)
    matches = [
        (seg_ext[tap_index : tap_index + t_dev] == seg_own).astype(jnp.float32)[:, None]
        for tap_index in range(KW)
    ]
    conv_out = jnp.zeros((t_dev, width), jnp.float32)
    for tap_index in range(KW):
        conv_out = (
            conv_out
            + kernel[tap_index] * glu_ext[tap_index : tap_index + t_dev] * matches[tap_index]
        )
    conv_out_grad = row_product(grad_out, lax.all_gather(w_conv_out, "dp", axis=0, tiled=True))
    conv_sig = jax.nn.sigmoid(conv_out)
    conv_grad = (conv_out_grad * conv_sig * (1.0 + conv_out * (1.0 - conv_sig))).astype(
        jnp.bfloat16
    )
    grad_ext = padded(conv_grad, (("seq", 0),), half).astype(jnp.float32)
    grad_float = grad_ext[half : half + t_dev]
    glu_grad = jnp.zeros((t_dev, width), jnp.float32)
    kernel_rows = []
    for tap_index in range(KW):
        back = 2 * half - tap_index
        glu_grad = glu_grad + kernel[tap_index] * grad_ext[back : back + t_dev] * matches[back]
        kernel_rows.append(
            jnp.sum(
                grad_float * glu_ext[tap_index : tap_index + t_dev] * matches[tap_index], axis=0
            )
        )
    glu_in_grad = jnp.concatenate(
        [glu_grad * gate_sig, glu_grad * first_half * gate_sig * (1.0 - gate_sig)], axis=1
    ).astype(jnp.bfloat16)
    norm_grad = row_product(glu_in_grad, lax.all_gather(w_in, "dp", axis=0, tiled=True))
    inputs = saved_input.astype(jnp.float32)
    centred = inputs - jnp.mean(inputs, axis=1, keepdims=True)
    inv_std = 1.0 / jnp.sqrt(jnp.mean(centred * centred, axis=1, keepdims=True) + 1e-05)
    normed = centred * inv_std
    scaled_grad = norm_grad * norm_gain
    input_grad = inv_std * (
        scaled_grad
        - jnp.mean(scaled_grad, axis=1, keepdims=True)
        - normed * jnp.mean(scaled_grad * normed, axis=1, keepdims=True)
    )
    resid_grad = (grad_out.astype(jnp.float32) + input_grad).astype(jnp.bfloat16)
    gain_term = jnp.sum(norm_grad * normed, axis=0)
    ctx_float = row_product(resid_grad, lax.all_gather(w_attn_out, "dp", axis=0, tiled=True))
    ctx_grad = ctx_float.astype(jnp.bfloat16)
    relayed = lax.all_to_all(ctx_grad, "seq", split_axis=1, concat_axis=0, tiled=True)
    seg_all = segments_of(frame_lens, jnp.arange(total, dtype=jnp.int32))
    query_grad, key_grad, value_grad = attention_backward(queries, keys, values, relayed, seg_all)
    kernel_grad, gain_grad = lax.psum((jnp.stack(kernel_rows), gain_term), ("dp", "seq"))
    return (resid_grad, query_grad, key_grad, value_grad, kernel_grad, gain_grad)


MESH = pl.DeviceIdType.MESH
NT = (((1,), (1,)), ((), ()))
NN = (((1,), (0,)), ((), ()))
TN = (((0,), (0,)), ((), ()))
PART = 48
LANES = 128
COPIES = 59


def fused(
    go_ref, x_ref, pre_ref, q_ref, k_ref, v_ref, counts_ref, gain_ref, kern_ref,
    w_in_ref, w_conv_ref, w_attn_ref,
    resid_ref, qg_ref, kg_ref, vg_ref, taps_ref, gaing_ref,
    full_conv, full_in, full_attn, glu_ref, gext_ref, halo_ref, seg_ref, segc_ref, mask_ref, kt_ref, vt_ref,
    conv_ref, cog_ref, cg_ref, cext_ref, gin_ref, ng_ref, probs_ref, ctx_ref, dout_ref,
    ka_ref, va_ref, sums_ref, part_a, mine_a, part_b, total_ref,
    send_sem, recv_sem, local_sem,
):
    f32, bf16 = jnp.float32, jnp.bfloat16
    rows, width = go_ref.shape
    cols, total = q_ref.shape
    heads = cols // HD
    n_seq = total // rows
    n_dp = 8
    shard = width // n_dp
    half = KW // 2
    me, z = lax.axis_index("dp"), lax.axis_index("seq")
    core = me % 2
    sib = me + 1 - 2 * core
    xn = me + 2 - 4 * ((me // 2) % 2)
    yn = me + 4 - 8 * (me // 4)
    diag = xn + 4 - 8 * (me // 4)
    over = 1 - 2 * core
    zn = z + 1 - 2 * (z % 2)
    moff = PART * (z % 2)
    toff = PART - moff

    barrier = pltpu.get_barrier_semaphore()
    for s in range(1, n_dp):
        pl.semaphore_signal(barrier, inc=1, device_id=((me + s) % n_dp, z), device_id_type=MESH)
    for s in range(1, n_seq):
        pl.semaphore_signal(barrier, inc=1, device_id=(me, (z + s) % n_seq), device_id_type=MESH)
    pl.semaphore_wait(barrier, n_dp + n_seq - 2)

    sent = []

    def remote(src, dst, idx, dp, seq):
        return pltpu.make_async_remote_copy(
            src_ref=src, dst_ref=dst, send_sem=send_sem.at[idx], recv_sem=recv_sem.at[idx],
            device_id=(dp, seq), device_id_type=MESH,
        )

    def push(src, dst, idx, dp, seq):
        copy = remote(src, dst, idx, dp, seq)
        copy.start()
        sent.append(copy)

    def arrive(dst, idx):
        remote(dst, dst, idx, sib, z).wait_recv()

    weights = ((w_conv_ref, full_conv), (w_in_ref, full_in), (w_attn_ref, full_attn))

    def span(start, size):
        return pl.ds(pl.multiple_of(start, 16), size)

    def piece(m, owner, off, size):
        return weights[m][1].at[span(owner * shard + off, size), :]

    rest = shard - 2 * PART
    own_copies = [
        pltpu.make_async_copy(weights[m][0], piece(m, me, 0, shard), local_sem.at[m])
        for m in range(3)
    ]

    def send_own(m):
        base = 13 * m
        source = weights[m][0]
        for k, dev in ((0, xn), (2, yn)):
            push(source.at[span(moff, PART), :], piece(m, me, moff, PART), base + k, dev, z)
            push(source.at[pl.ds(2 * PART, rest), :], piece(m, me, 2 * PART, rest), base + k + 1, dev, z)
        push(source, piece(m, me, 0, shard), base + 9, sib, z)
        own_copies[m].start()

    def forward_xy(m):
        base = 13 * m
        for k, dev in ((0, xn), (2, yn)):
            arrive(piece(m, dev, moff, PART), base + k)
            arrive(piece(m, dev, 2 * PART, rest), base + k + 1)
        via = core * yn + (1 - core) * xn
        owner = core * xn + (1 - core) * yn
        for k, off, size in ((4, moff, PART), (5, 2 * PART, rest)):
            push(piece(m, owner, off, size), piece(m, owner, off, size), base + k, via, z)
        for k, dev in ((6, xn), (7, yn)):
            push(piece(m, dev, moff, PART), piece(m, dev, moff, PART), base + k, me, zn)

    def forward_diag(m):
        base = 13 * m
        arrive(piece(m, diag, moff, PART), base + 4)
        push(piece(m, diag, moff, PART), piece(m, diag, moff, PART), base + 8, me, zn)
        arrive(piece(m, diag, 2 * PART, rest), base + 5)

    def forward_sib(m):
        base = 13 * m
        for k, dev in ((6, xn), (7, yn)):
            arrive(piece(m, dev, toff, PART), base + k)
            push(piece(m, dev, 0, shard), piece(m, dev, 0, shard), base + k + 4, sib, z)

    def finish(m):
        base = 13 * m
        arrive(piece(m, diag, toff, PART), base + 8)
        push(piece(m, diag, 0, shard), piece(m, diag, 0, shard), base + 12, sib, z)
        for k, dev in ((9, sib), (10, xn + over), (11, yn + over), (12, diag + over)):
            arrive(piece(m, dev, 0, shard), base + k)
        own_copies[m].wait()

    def segments(pos):
        end = jnp.int32(0)
        seg = jnp.zeros(pos.shape, jnp.int32)
        for u in range(counts_ref.shape[1]):
            end = end + counts_ref[0, u]
            seg = seg + jnp.where(pos >= end, 1, 0)
        return jnp.where(pos < 0, -1, seg)

    def tiles(n, size):
        return pl.ds(pl.multiple_of(n * size, size), size)

    prev, following = (z + n_seq - 1) % n_seq, (z + 1) % n_seq

    def send_halo(src, slot, idx):
        push(src.at[pl.ds(rows - 16, 16), :], halo_ref.at[slot], idx, me, following)
        push(src.at[pl.ds(0, 16), :], halo_ref.at[slot + 1], idx + 1, me, prev)

    def take_halo(dst, slot, idx):
        arrive(halo_ref.at[slot], idx)
        arrive(halo_ref.at[slot + 1], idx + 1)
        dst[0:16, :] = halo_ref[slot].astype(f32)
        dst[rows + 16 : rows + 32, :] = halo_ref[slot + 1].astype(f32)

    send_own(0)
    send_own(1)

    @pl.loop(0, width // LANES)
    def _(n):
        c = tiles(n, LANES)
        c2 = pl.ds(pl.multiple_of(width + n * LANES, LANES), LANES)
        gate = jax.nn.sigmoid(pre_ref[:, c2].astype(f32))
        glu = (pre_ref[:, c].astype(f32) * gate).astype(bf16)
        glu_ref[:, c] = glu
        gext_ref[16 : 16 + rows, c] = glu.astype(f32)

    send_halo(glu_ref, 0, 39)

    seg_ref[...] = segments(
        z * rows - 16 + lax.broadcasted_iota(jnp.int32, (rows + 32, LANES), 0)
    )
    segc_ref[...] = segments(lax.broadcasted_iota(jnp.int32, (total, LANES), 0))
    for o in range(KW):
        same = seg_ref[o + 1 : o + 1 + rows, :] == seg_ref[16 : 16 + rows, :]
        mask_ref[o] = jnp.where(same, 1.0, 0.0)

    scale = 1.0 / math.sqrt(HD)
    qblock = 256

    def head(h):
        return pl.ds(pl.multiple_of(h * HD, 16), HD)

    def make_probs(h):
        keys = k_ref[head(h), :].astype(f32).T.astype(bf16)
        kt_ref[...] = keys
        vt_ref[h] = v_ref[head(h), :].astype(f32).T.astype(bf16)

        @pl.loop(0, total // qblock)
        def _(b):
            scores = (
                lax.dot_general(
                    kt_ref[...], q_ref[head(h), tiles(b, qblock)], NN, preferred_element_type=f32
                )
                * scale
            )
            seg_q = segments(b * qblock + lax.broadcasted_iota(jnp.int32, (1, qblock), 1))
            seg_k = jnp.concatenate([segc_ref[...]] * (qblock // LANES), axis=1)
            scores = jnp.where(seg_k == seg_q, scores, -1e30)
            expd = jnp.exp(scores - jnp.max(scores, axis=0, keepdims=True))
            probs_ref[h, b] = expd * (1.0 / jnp.sum(expd, axis=0, keepdims=True))

    make_probs(0)
    forward_xy(0)
    send_own(2)

    take_halo(gext_ref, 0, 39)
    reach = rows // 2 + 24

    def taps(r):
        return [(o, o + 1 - r) for o in range(KW) if (o + 1) % 8 == r]

    @pl.loop(0, width // LANES)
    def _(n):
        c = tiles(n, LANES)
        for low in (0, rows // 2):
            acc = jnp.zeros((rows // 2, LANES), f32)
            for r in range(8):
                near = gext_ref[low + r : low + r + reach, c]
                for o, at in taps(r):
                    here = near[at : at + rows // 2] * mask_ref[o, low : low + rows // 2, :]
                    acc = acc + kern_ref[o : o + 1, c] * here
            conv_ref[low : low + rows // 2, c] = acc

    forward_diag(0)

    @pl.loop(1, heads - 1)
    def _(h):
        make_probs(h)

    forward_sib(0)
    make_probs(heads - 1)
    finish(0)

    @pl.loop(0, width // 256)
    def _(n):
        c = tiles(n, 256)
        cog_ref[:, c] = lax.dot_general(go_ref[...], full_conv[c, :], NT, preferred_element_type=f32)

    @pl.loop(0, width // LANES)
    def _(n):
        c = tiles(n, LANES)
        conv = conv_ref[:, c]
        sig = jax.nn.sigmoid(conv)
        grad = (cog_ref[:, c] * sig * (1.0 + conv * (1.0 - sig))).astype(bf16)
        cg_ref[:, c] = grad
        cext_ref[16 : 16 + rows, c] = grad.astype(f32)

    send_halo(cg_ref, 2, 41)
    take_halo(cext_ref, 2, 41)

    def back(first, last):
        @pl.loop(first, last)
        def _(n):
            c = tiles(n, LANES)
            c2 = pl.ds(pl.multiple_of(width + n * LANES, LANES), LANES)
            for low in (0, rows // 2):
                part = pl.ds(low, rows // 2)
                grad_own = cext_ref[low + 16 : low + 16 + rows // 2, c]
                acc = jnp.zeros((rows // 2, LANES), f32)
                for r in range(8):
                    near_c = cext_ref[low + r : low + r + reach, c]
                    near_g = gext_ref[low + r : low + r + reach, c]
                    for o, at in taps(r):
                        mask = mask_ref[o, part, :]
                        acc = acc + kern_ref[KW - 1 - o : KW - o, c] * (
                            near_c[at : at + rows // 2] * mask
                        )
                        pair = grad_own * (near_g[at : at + rows // 2] * mask)
                        pair = jnp.sum(pair, axis=0, keepdims=True)
                        if low == 0:
                            sums_ref[o : o + 1, c] = pair
                        else:
                            sums_ref[o : o + 1, c] += pair
                gate = jax.nn.sigmoid(pre_ref[part, c2].astype(f32))
                scaled = acc * gate
                gin_ref[part, c] = scaled.astype(bf16)
                gin_ref[part, c2] = (scaled * pre_ref[part, c].astype(f32) * (1.0 - gate)).astype(bf16)

    blocks = width // LANES
    forward_xy(1)
    back(0, blocks * 2 // 5)
    forward_diag(1)
    back(blocks * 2 // 5, blocks * 7 // 10)
    forward_xy(2)
    back(blocks * 7 // 10, blocks)
    forward_sib(1)
    forward_diag(2)
    finish(1)

    @pl.loop(0, width // 256)
    def _(n):
        c = tiles(n, 256)
        ng_ref[:, c] = lax.dot_general(gin_ref[...], full_in[c, :], NT, preferred_element_type=f32)

    forward_sib(2)
    sums_ref[KW : KW + 1, :] = jnp.zeros((1, width), f32)
    gain = gain_ref[...].reshape(1, width)

    @pl.loop(0, rows // 16)
    def _(n):
        r = tiles(n, 16)
        x = x_ref[r, :].astype(f32)
        centred = x - jnp.mean(x, axis=1, keepdims=True)
        inv = 1.0 / jnp.sqrt(jnp.mean(centred * centred, axis=1, keepdims=True) + 1e-05)
        normed = centred * inv
        grad = ng_ref[r, :]
        scaled = grad * gain
        back = inv * (
            scaled
            - jnp.mean(scaled, axis=1, keepdims=True)
            - normed * jnp.mean(scaled * normed, axis=1, keepdims=True)
        )
        resid_ref[r, :] = (go_ref[r, :].astype(f32) + back).astype(bf16)
        sums_ref[KW : KW + 1, :] += jnp.sum(grad * normed, axis=0, keepdims=True)

    for s in range(1, n_seq):
        to = (z + s) % n_seq
        push(sums_ref.at[tiles(to, 8), :], part_a.at[s - 1], 45 + s, me, to)
    finish(2)

    for s in range(1, n_seq + 1):
        to = (z + s) % n_seq
        out = lax.dot_general(
            full_attn[tiles(to, cols), :], resid_ref[...], NT, preferred_element_type=f32
        ).astype(bf16)
        if s < n_seq:
            ctx_ref[s - 1] = out
            push(ctx_ref.at[s - 1], dout_ref.at[z], 42 + s, me, to)
        else:
            dout_ref[z] = out

    for s in range(1, n_seq):
        arrive(part_a.at[s - 1], 45 + s)
    mine_a[...] = sums_ref[tiles(z, 8), :] + part_a[0] + part_a[1] + part_a[2]
    for s in range(1, n_dp):
        push(mine_a, part_b.at[me], 48 + s, (me + s) % n_dp, z)
    part_b[me] = mine_a[...]

    for s in range(1, n_seq):
        arrive(dout_ref.at[(z + n_seq - s) % n_seq], 42 + s)

    def attend(first, last):
        @pl.loop(first, last)
        def _(h):
            hd = head(h)
            per = qblock // rows
            for b in range(total // qblock):
                q = pl.ds(b * qblock, qblock)
                probs = probs_ref[h, b]
                dout = jnp.concatenate(
                    [dout_ref[b * per + i, hd, :] for i in range(per)], axis=1
                )
                prob_grad = lax.dot_general(vt_ref[h], dout, NN, preferred_element_type=f32)
                delta = jnp.sum(probs * prob_grad, axis=0, keepdims=True)
                score_grad = (probs * (prob_grad - delta)).astype(bf16)
                value_part = lax.dot_general(dout, probs.astype(bf16), NT, preferred_element_type=f32)
                key_part = lax.dot_general(q_ref[hd, q], score_grad, NT, preferred_element_type=f32)
                query_part = lax.dot_general(k_ref[hd, :], score_grad, NN, preferred_element_type=f32)
                qg_ref[hd, q] = (query_part * scale).astype(bf16)
                if b == 0:
                    va_ref[...] = value_part
                    ka_ref[...] = key_part
                else:
                    va_ref[...] += value_part
                    ka_ref[...] += key_part
            kg_ref[hd, :] = (ka_ref[...] * scale).astype(bf16)
            vg_ref[hd, :] = va_ref[...].astype(bf16)

    attend(0, heads // 2)
    for s in range(1, n_dp):
        arrive(part_b.at[(me + n_dp - s) % n_dp], 48 + s)
    chunk = part_b[0]
    for i in range(1, n_dp):
        chunk = chunk + part_b[i]
    total_ref[tiles(z, 8), :] = chunk
    for s in range(1, n_seq):
        block = total_ref.at[tiles(z, 8), :]
        push(block, block, 55 + s, me, (z + s) % n_seq)
    attend(heads // 2, heads)

    for s in range(1, n_seq):
        arrive(total_ref.at[tiles((z + n_seq - s) % n_seq, 8), :], 55 + s)
    taps_ref[...] = total_ref[0:KW, :]
    gaing_ref[...] = total_ref[KW : KW + 1, :].reshape(width)
    for copy in sent:
        copy.wait_send()


def fused_local(
    grad_out, saved_input, pre_glu, queries, keys, values, frame_counts, norm_gain, kernel,
    w_in, w_conv_out, w_attn_out,
):
    rows, width = grad_out.shape
    total, cols = queries.shape
    queries, keys, values = queries.T, keys.T, values.T
    heads = cols // HD
    f32, bf16 = jnp.float32, jnp.bfloat16
    vmem = pl.BlockSpec(memory_space=pltpu.VMEM)
    smem = pl.BlockSpec(memory_space=pltpu.SMEM)
    hbm = pl.BlockSpec(memory_space=pl.ANY)
    outs = pl.pallas_call(
        fused,
        out_shape=(
            jax.ShapeDtypeStruct((rows, width), bf16),
            jax.ShapeDtypeStruct((cols, total), bf16),
            jax.ShapeDtypeStruct((cols, total), bf16),
            jax.ShapeDtypeStruct((cols, total), bf16),
            jax.ShapeDtypeStruct((KW, width), f32),
            jax.ShapeDtypeStruct((width,), f32),
        ),
        in_specs=[vmem] * 6 + [smem] + [vmem] * 2 + [hbm] * 3,
        out_specs=(vmem,) * 6,
        scratch_shapes=[
            pltpu.VMEM((width, width), bf16),
            pltpu.VMEM((width, 2 * width), bf16),
            pltpu.VMEM((width, width), bf16),
            pltpu.VMEM((rows, width), bf16),
            pltpu.VMEM((rows + 32, width), f32),
            pltpu.VMEM((4, 16, width), bf16),
            pltpu.VMEM((rows + 32, LANES), jnp.int32),
            pltpu.VMEM((total, LANES), jnp.int32),
            pltpu.VMEM((KW, rows, LANES), f32),
            pltpu.VMEM((total, HD), bf16),
            pltpu.VMEM((heads, total, HD), bf16),
            pltpu.VMEM((rows, width), f32),
            pltpu.VMEM((rows, width), f32),
            pltpu.VMEM((rows, width), bf16),
            pltpu.VMEM((rows + 32, width), f32),
            pltpu.VMEM((rows, 2 * width), bf16),
            pltpu.VMEM((rows, width), f32),
            pltpu.VMEM((heads, total // 256, total, 256), f32),
            pltpu.VMEM((3, cols, rows), bf16),
            pltpu.VMEM((4, cols, rows), bf16),
            pltpu.VMEM((HD, total), f32),
            pltpu.VMEM((HD, total), f32),
            pltpu.VMEM((KW + 1, width), f32),
            pltpu.VMEM((3, 8, width), f32),
            pltpu.VMEM((8, width), f32),
            pltpu.VMEM((8, 8, width), f32),
            pltpu.VMEM((KW + 1, width), f32),
            pltpu.SemaphoreType.DMA((COPIES,)),
            pltpu.SemaphoreType.DMA((COPIES,)),
            pltpu.SemaphoreType.DMA((3,)),
        ],
        compiler_params=pltpu.CompilerParams(
            collective_id=0, has_side_effects=True, vmem_limit_bytes=50 * 1024 * 1024
        ),
    )(
        grad_out, saved_input, pre_glu, queries, keys, values, frame_counts,
        norm_gain, kernel, w_in, w_conv_out, w_attn_out,
    )
    return (outs[0], outs[1].T, outs[2].T, outs[3].T, outs[4], outs[5])


def solution(mesh):
    in_specs = (
        P(("dp", "seq"), None),
        P(("dp", "seq"), None),
        P(("dp", "seq"), None),
        P("dp", "seq"),
        P("dp", "seq"),
        P("dp", "seq"),
        P("dp", None),
        P(),
        P(),
        P("dp", None),
        P("dp", None),
        P("dp", None),
    )
    out_specs = (P(("dp", "seq"), None), P("dp", "seq"), P("dp", "seq"), P("dp", "seq"), P(), P())
    small = mesh.shape["dp"] == 8 and mesh.shape["seq"] == 4
    body = fused_local if small else local
    return jax.shard_map(body, mesh=mesh, in_specs=in_specs, out_specs=out_specs, check_vma=False)
```

```python
import math

import jax
import jax.numpy as jnp
from jax import lax
from jax.experimental import pallas as pl
from jax.experimental.pallas import tpu as pltpu
from jax.sharding import PartitionSpec as P

HD = 80
KW = 31


def padded(block, sides, width):
    for axis, dim in sides:
        count = lax.axis_size(axis)
        forward = [(i, i + 1) for i in range(count - 1)]
        backward = [(target, source) for source, target in forward]
        low = lax.ppermute(
            lax.slice_in_dim(block, block.shape[dim] - width, None, axis=dim), axis, forward
        )
        high = lax.ppermute(lax.slice_in_dim(block, 0, width, axis=dim), axis, backward)
        block = jnp.concatenate([low, block, high], axis=dim)
    return block


def segments_of(frame_lens, positions):
    ends = jnp.cumsum(frame_lens)
    counted = jnp.sum((positions[:, None] >= ends[None, :]).astype(jnp.int32), axis=1)
    return jnp.where(positions < 0, jnp.int32(-1), counted)


def row_product(active, piece):
    return jnp.einsum("tc,rc->tr", active, piece, preferred_element_type=jnp.float32)


def attention_backward(query_rows, key_rows, value_rows, out_grad, seg_all):
    total, columns = query_rows.shape
    heads = columns // HD
    scale = 1.0 / math.sqrt(HD)
    query_heads = query_rows.reshape(total, heads, HD)
    key_heads = key_rows.reshape(total, heads, HD)
    value_heads = value_rows.reshape(total, heads, HD)
    grad_heads = out_grad.reshape(total, heads, HD)
    qblock = min(512, total)
    nblocks = total // qblock

    def block_step(block, carry):
        query_out, key_acc, value_acc = carry
        qstart = block * qblock
        query_block = lax.dynamic_slice_in_dim(query_heads, qstart, qblock, 0)
        grad_block = lax.dynamic_slice_in_dim(grad_heads, qstart, qblock, 0)
        seg_query = lax.dynamic_slice_in_dim(seg_all, qstart, qblock, 0)
        scores = (
            jnp.einsum("qhd,khd->hqk", query_block, key_heads, preferred_element_type=jnp.float32)
            * scale
        )
        scores = jnp.where((seg_query[:, None] == seg_all[None, :])[None], scores, -1e30)
        peak = jnp.max(scores, axis=2, keepdims=True)
        expd = jnp.exp(scores - peak)
        probs = expd / jnp.sum(expd, axis=2, keepdims=True)
        probs_low = probs.astype(jnp.bfloat16)
        value_part = jnp.einsum(
            "hqk,qhd->khd", probs_low, grad_block, preferred_element_type=jnp.float32
        )
        prob_grad = jnp.einsum(
            "qhd,khd->hqk", grad_block, value_heads, preferred_element_type=jnp.float32
        )
        delta = jnp.sum(probs * prob_grad, axis=2, keepdims=True)
        score_grad = (probs * (prob_grad - delta)).astype(jnp.bfloat16)
        query_part = (
            jnp.einsum("hqk,khd->qhd", score_grad, key_heads, preferred_element_type=jnp.float32)
            * scale
        ).astype(jnp.bfloat16)
        key_part = jnp.einsum(
            "hqk,qhd->khd", score_grad, query_block, preferred_element_type=jnp.float32
        )
        query_out = lax.dynamic_update_slice_in_dim(query_out, query_part, qstart, 0)
        return (query_out, key_acc + key_part, value_acc + value_part)

    initial = (
        jnp.zeros((total, heads, HD), jnp.bfloat16),
        jnp.zeros((total, heads, HD), jnp.float32),
        jnp.zeros((total, heads, HD), jnp.float32),
    )
    query_out, key_acc, value_acc = lax.fori_loop(0, nblocks, block_step, initial)
    key_grad = (key_acc * scale).astype(jnp.bfloat16)
    value_grad = value_acc.astype(jnp.bfloat16)
    return (
        query_out.reshape(total, columns),
        key_grad.reshape(total, columns),
        value_grad.reshape(total, columns),
    )


def local(
    grad_out,
    saved_input,
    pre_glu,
    queries,
    keys,
    values,
    frame_counts,
    norm_gain,
    kernel,
    w_in,
    w_conv_out,
    w_attn_out,
):
    t_dev, width = grad_out.shape
    n_seq = lax.axis_size("seq")
    total = t_dev * n_seq
    half = KW // 2
    frame_lens = frame_counts[0]
    seq_index = lax.axis_index("seq")
    ext_pos = seq_index * t_dev + jnp.arange(-half, t_dev + half, dtype=jnp.int32)
    seg_ext = segments_of(frame_lens, ext_pos)
    seg_own = seg_ext[half : half + t_dev]
    first_half = pre_glu[:, :width].astype(jnp.float32)
    gate_sig = jax.nn.sigmoid(pre_glu[:, width:].astype(jnp.float32))
    glu_out = (first_half * gate_sig).astype(jnp.bfloat16)
    glu_ext = padded(glu_out, (("seq", 0),), half).astype(jnp.float32)
    matches = [
        (seg_ext[tap_index : tap_index + t_dev] == seg_own).astype(jnp.float32)[:, None]
        for tap_index in range(KW)
    ]
    conv_out = jnp.zeros((t_dev, width), jnp.float32)
    for tap_index in range(KW):
        conv_out = (
            conv_out
            + kernel[tap_index] * glu_ext[tap_index : tap_index + t_dev] * matches[tap_index]
        )
    conv_out_grad = row_product(grad_out, lax.all_gather(w_conv_out, "dp", axis=0, tiled=True))
    conv_sig = jax.nn.sigmoid(conv_out)
    conv_grad = (conv_out_grad * conv_sig * (1.0 + conv_out * (1.0 - conv_sig))).astype(
        jnp.bfloat16
    )
    grad_ext = padded(conv_grad, (("seq", 0),), half).astype(jnp.float32)
    grad_float = grad_ext[half : half + t_dev]
    glu_grad = jnp.zeros((t_dev, width), jnp.float32)
    kernel_rows = []
    for tap_index in range(KW):
        back = 2 * half - tap_index
        glu_grad = glu_grad + kernel[tap_index] * grad_ext[back : back + t_dev] * matches[back]
        kernel_rows.append(
            jnp.sum(
                grad_float * glu_ext[tap_index : tap_index + t_dev] * matches[tap_index], axis=0
            )
        )
    glu_in_grad = jnp.concatenate(
        [glu_grad * gate_sig, glu_grad * first_half * gate_sig * (1.0 - gate_sig)], axis=1
    ).astype(jnp.bfloat16)
    norm_grad = row_product(glu_in_grad, lax.all_gather(w_in, "dp", axis=0, tiled=True))
    inputs = saved_input.astype(jnp.float32)
    centred = inputs - jnp.mean(inputs, axis=1, keepdims=True)
    inv_std = 1.0 / jnp.sqrt(jnp.mean(centred * centred, axis=1, keepdims=True) + 1e-05)
    normed = centred * inv_std
    scaled_grad = norm_grad * norm_gain
    input_grad = inv_std * (
        scaled_grad
        - jnp.mean(scaled_grad, axis=1, keepdims=True)
        - normed * jnp.mean(scaled_grad * normed, axis=1, keepdims=True)
    )
    resid_grad = (grad_out.astype(jnp.float32) + input_grad).astype(jnp.bfloat16)
    gain_term = jnp.sum(norm_grad * normed, axis=0)
    ctx_float = row_product(resid_grad, lax.all_gather(w_attn_out, "dp", axis=0, tiled=True))
    ctx_grad = ctx_float.astype(jnp.bfloat16)
    relayed = lax.all_to_all(ctx_grad, "seq", split_axis=1, concat_axis=0, tiled=True)
    seg_all = segments_of(frame_lens, jnp.arange(total, dtype=jnp.int32))
    query_grad, key_grad, value_grad = attention_backward(queries, keys, values, relayed, seg_all)
    kernel_grad, gain_grad = lax.psum((jnp.stack(kernel_rows), gain_term), ("dp", "seq"))
    return (resid_grad, query_grad, key_grad, value_grad, kernel_grad, gain_grad)


MESH = pl.DeviceIdType.MESH
NT = (((1,), (1,)), ((), ()))
NN = (((1,), (0,)), ((), ()))
TN = (((0,), (0,)), ((), ()))
PART = 48
LANES = 128
COPIES = 59


def fused(
    go_hbm, x_hbm, pre_hbm, q_hbm, k_hbm, v_hbm, counts_ref, gain_hbm, kern_hbm,
    w_in_ref, w_conv_ref, w_attn_ref,
    resid_ref, qg_ref, kg_ref, vg_ref, taps_ref, gaing_ref,
    full_conv, full_in, full_attn, glu_ref, gext_ref, halo_ref, seg_ref, segc_ref, mask_ref, kt_ref, vt_ref,
    conv_ref, cog_ref, cg_ref, cext_ref, gin_ref, ng_ref, probs_ref, ctx_ref, dout_ref,
    ka_ref, va_ref, sums_ref, part_a, mine_a, part_b, total_ref,
    go_ref, x_ref, pre_ref, q_ref, k_ref, v_ref, gain_ref, kern_ref,
    send_sem, recv_sem, local_sem,
):
    f32, bf16 = jnp.float32, jnp.bfloat16
    rows, width = go_ref.shape
    cols, total = q_ref.shape
    heads = cols // HD
    n_seq = total // rows
    n_dp = 8
    shard = width // n_dp
    half = KW // 2
    me, z = lax.axis_index("dp"), lax.axis_index("seq")
    core = me % 2
    sib = me + 1 - 2 * core
    xn = me + 2 - 4 * ((me // 2) % 2)
    yn = me + 4 - 8 * (me // 4)
    diag = xn + 4 - 8 * (me // 4)
    over = 1 - 2 * core
    zn = z + 1 - 2 * (z % 2)
    moff = PART * (z % 2)
    toff = PART - moff

    loads = [
        pltpu.make_async_copy(source, target, local_sem.at[3 + i])
        for i, (source, target) in enumerate((
            (pre_hbm, pre_ref), (k_hbm, k_ref), (q_hbm, q_ref), (v_hbm, v_ref),
            (kern_hbm, kern_ref), (go_hbm, go_ref), (x_hbm, x_ref), (gain_hbm, gain_ref),
        ))
    ]
    for load in loads:
        load.start()

    barrier = pltpu.get_barrier_semaphore()
    for s in range(1, n_dp):
        pl.semaphore_signal(barrier, inc=1, device_id=((me + s) % n_dp, z), device_id_type=MESH)
    for s in range(1, n_seq):
        pl.semaphore_signal(barrier, inc=1, device_id=(me, (z + s) % n_seq), device_id_type=MESH)
    pl.semaphore_wait(barrier, n_dp + n_seq - 2)

    sent = []

    def remote(src, dst, idx, dp, seq):
        return pltpu.make_async_remote_copy(
            src_ref=src, dst_ref=dst, send_sem=send_sem.at[idx], recv_sem=recv_sem.at[idx],
            device_id=(dp, seq), device_id_type=MESH,
        )

    def push(src, dst, idx, dp, seq):
        copy = remote(src, dst, idx, dp, seq)
        copy.start()
        sent.append(copy)

    def arrive(dst, idx):
        remote(dst, dst, idx, sib, z).wait_recv()

    weights = ((w_conv_ref, full_conv), (w_in_ref, full_in), (w_attn_ref, full_attn))

    def span(start, size):
        return pl.ds(pl.multiple_of(start, 16), size)

    def piece(m, owner, off, size):
        return weights[m][1].at[span(owner * shard + off, size), :]

    rest = shard - 2 * PART
    own_copies = [
        pltpu.make_async_copy(weights[m][0], piece(m, me, 0, shard), local_sem.at[m])
        for m in range(3)
    ]

    def send_own(m):
        base = 13 * m
        source = weights[m][0]
        for k, dev in ((0, xn), (2, yn)):
            push(source.at[span(moff, PART), :], piece(m, me, moff, PART), base + k, dev, z)
            push(source.at[pl.ds(2 * PART, rest), :], piece(m, me, 2 * PART, rest), base + k + 1, dev, z)
        push(source, piece(m, me, 0, shard), base + 9, sib, z)
        own_copies[m].start()

    def forward_xy(m):
        base = 13 * m
        for k, dev in ((0, xn), (2, yn)):
            arrive(piece(m, dev, moff, PART), base + k)
            arrive(piece(m, dev, 2 * PART, rest), base + k + 1)
        via = core * yn + (1 - core) * xn
        owner = core * xn + (1 - core) * yn
        for k, off, size in ((4, moff, PART), (5, 2 * PART, rest)):
            push(piece(m, owner, off, size), piece(m, owner, off, size), base + k, via, z)
        for k, dev in ((6, xn), (7, yn)):
            push(piece(m, dev, moff, PART), piece(m, dev, moff, PART), base + k, me, zn)

    def forward_diag(m):
        base = 13 * m
        arrive(piece(m, diag, moff, PART), base + 4)
        push(piece(m, diag, moff, PART), piece(m, diag, moff, PART), base + 8, me, zn)
        arrive(piece(m, diag, 2 * PART, rest), base + 5)

    def forward_sib(m):
        base = 13 * m
        for k, dev in ((6, xn), (7, yn)):
            arrive(piece(m, dev, toff, PART), base + k)
            push(piece(m, dev, 0, shard), piece(m, dev, 0, shard), base + k + 4, sib, z)

    def finish(m):
        base = 13 * m
        arrive(piece(m, diag, toff, PART), base + 8)
        push(piece(m, diag, 0, shard), piece(m, diag, 0, shard), base + 12, sib, z)
        for k, dev in ((9, sib), (10, xn + over), (11, yn + over), (12, diag + over)):
            arrive(piece(m, dev, 0, shard), base + k)
        own_copies[m].wait()

    def segments(pos):
        end = jnp.int32(0)
        seg = jnp.zeros(pos.shape, jnp.int32)
        for u in range(counts_ref.shape[1]):
            end = end + counts_ref[0, u]
            seg = seg + jnp.where(pos >= end, 1, 0)
        return jnp.where(pos < 0, -1, seg)

    def tiles(n, size):
        return pl.ds(pl.multiple_of(n * size, size), size)

    prev, following = (z + n_seq - 1) % n_seq, (z + 1) % n_seq

    def send_halo(src, slot, idx):
        push(src.at[pl.ds(rows - 16, 16), :], halo_ref.at[slot], idx, me, following)
        push(src.at[pl.ds(0, 16), :], halo_ref.at[slot + 1], idx + 1, me, prev)

    def take_halo(dst, slot, idx):
        arrive(halo_ref.at[slot], idx)
        arrive(halo_ref.at[slot + 1], idx + 1)
        dst[0:16, :] = halo_ref[slot].astype(f32)
        dst[rows + 16 : rows + 32, :] = halo_ref[slot + 1].astype(f32)

    send_own(0)
    loads[0].wait()

    @pl.loop(0, width // LANES)
    def _(n):
        c = tiles(n, LANES)
        c2 = pl.ds(pl.multiple_of(width + n * LANES, LANES), LANES)
        gate = jax.nn.sigmoid(pre_ref[:, c2].astype(f32))
        glu = (pre_ref[:, c].astype(f32) * gate).astype(bf16)
        glu_ref[:, c] = glu
        gext_ref[16 : 16 + rows, c] = glu.astype(f32)

    send_halo(glu_ref, 0, 39)

    seg_ref[...] = segments(
        z * rows - 16 + lax.broadcasted_iota(jnp.int32, (rows + 32, LANES), 0)
    )
    segc_ref[...] = segments(lax.broadcasted_iota(jnp.int32, (total, LANES), 0))
    for o in range(KW):
        same = seg_ref[o + 1 : o + 1 + rows, :] == seg_ref[16 : 16 + rows, :]
        mask_ref[o] = jnp.where(same, 1.0, 0.0)

    scale = 1.0 / math.sqrt(HD)
    qblock = 256

    def head(h):
        return pl.ds(pl.multiple_of(h * HD, 16), HD)

    def make_probs(h):
        keys = k_ref[head(h), :].astype(f32).T.astype(bf16)
        kt_ref[...] = keys
        vt_ref[h] = v_ref[head(h), :].astype(f32).T.astype(bf16)

        @pl.loop(0, total // qblock)
        def _(b):
            scores = (
                lax.dot_general(
                    kt_ref[...], q_ref[head(h), tiles(b, qblock)], NN, preferred_element_type=f32
                )
                * scale
            )
            seg_q = segments(b * qblock + lax.broadcasted_iota(jnp.int32, (1, qblock), 1))
            seg_k = jnp.concatenate([segc_ref[...]] * (qblock // LANES), axis=1)
            scores = jnp.where(seg_k == seg_q, scores, -1e30)
            expd = jnp.exp(scores - jnp.max(scores, axis=0, keepdims=True))
            probs_ref[h, b] = expd * (1.0 / jnp.sum(expd, axis=0, keepdims=True))

    for load in loads[1:]:
        load.wait()
    make_probs(0)
    forward_xy(0)
    send_own(1)

    take_halo(gext_ref, 0, 39)
    reach = rows // 2 + 24

    def taps(r):
        return [(o, o + 1 - r) for o in range(KW) if (o + 1) % 8 == r]

    @pl.loop(0, width // LANES)
    def _(n):
        c = tiles(n, LANES)
        for low in (0, rows // 2):
            acc = jnp.zeros((rows // 2, LANES), f32)
            for r in range(8):
                near = gext_ref[low + r : low + r + reach, c]
                for o, at in taps(r):
                    here = near[at : at + rows // 2] * mask_ref[o, low : low + rows // 2, :]
                    acc = acc + kern_ref[o : o + 1, c] * here
            conv_ref[low : low + rows // 2, c] = acc

    forward_diag(0)

    @pl.loop(1, heads - 1)
    def _(h):
        make_probs(h)

    forward_sib(0)
    make_probs(heads - 1)
    finish(0)

    @pl.loop(0, width // 256)
    def _(n):
        c = tiles(n, 256)
        cog_ref[:, c] = lax.dot_general(go_ref[...], full_conv[c, :], NT, preferred_element_type=f32)

    @pl.loop(0, width // LANES)
    def _(n):
        c = tiles(n, LANES)
        conv = conv_ref[:, c]
        sig = jax.nn.sigmoid(conv)
        grad = (cog_ref[:, c] * sig * (1.0 + conv * (1.0 - sig))).astype(bf16)
        cg_ref[:, c] = grad
        cext_ref[16 : 16 + rows, c] = grad.astype(f32)

    send_halo(cg_ref, 2, 41)
    take_halo(cext_ref, 2, 41)

    def back(first, last):
        @pl.loop(first, last)
        def _(n):
            c = tiles(n, LANES)
            c2 = pl.ds(pl.multiple_of(width + n * LANES, LANES), LANES)
            for low in (0, rows // 2):
                part = pl.ds(low, rows // 2)
                grad_own = cext_ref[low + 16 : low + 16 + rows // 2, c]
                acc = jnp.zeros((rows // 2, LANES), f32)
                for r in range(8):
                    near_c = cext_ref[low + r : low + r + reach, c]
                    near_g = gext_ref[low + r : low + r + reach, c]
                    for o, at in taps(r):
                        mask = mask_ref[o, part, :]
                        acc = acc + kern_ref[KW - 1 - o : KW - o, c] * (
                            near_c[at : at + rows // 2] * mask
                        )
                        pair = grad_own * (near_g[at : at + rows // 2] * mask)
                        pair = jnp.sum(pair, axis=0, keepdims=True)
                        if low == 0:
                            sums_ref[o : o + 1, c] = pair
                        else:
                            sums_ref[o : o + 1, c] += pair
                gate = jax.nn.sigmoid(pre_ref[part, c2].astype(f32))
                scaled = acc * gate
                gin_ref[part, c] = scaled.astype(bf16)
                gin_ref[part, c2] = (scaled * pre_ref[part, c].astype(f32) * (1.0 - gate)).astype(bf16)

    blocks = width // LANES
    forward_xy(1)
    send_own(2)
    back(0, blocks * 2 // 5)
    forward_diag(1)
    back(blocks * 2 // 5, blocks * 7 // 10)
    forward_xy(2)
    back(blocks * 7 // 10, blocks)
    forward_sib(1)
    forward_diag(2)
    finish(1)

    @pl.loop(0, width // 256)
    def _(n):
        c = tiles(n, 256)
        ng_ref[:, c] = lax.dot_general(gin_ref[...], full_in[c, :], NT, preferred_element_type=f32)

    forward_sib(2)
    sums_ref[KW : KW + 1, :] = jnp.zeros((1, width), f32)
    gain = gain_ref[...].reshape(1, width)

    @pl.loop(0, rows // 16)
    def _(n):
        r = tiles(n, 16)
        x = x_ref[r, :].astype(f32)
        centred = x - jnp.mean(x, axis=1, keepdims=True)
        inv = 1.0 / jnp.sqrt(jnp.mean(centred * centred, axis=1, keepdims=True) + 1e-05)
        normed = centred * inv
        grad = ng_ref[r, :]
        scaled = grad * gain
        back = inv * (
            scaled
            - jnp.mean(scaled, axis=1, keepdims=True)
            - normed * jnp.mean(scaled * normed, axis=1, keepdims=True)
        )
        resid_ref[r, :] = (go_ref[r, :].astype(f32) + back).astype(bf16)
        sums_ref[KW : KW + 1, :] += jnp.sum(grad * normed, axis=0, keepdims=True)

    for s in range(1, n_seq):
        to = (z + s) % n_seq
        push(sums_ref.at[tiles(to, 8), :], part_a.at[s - 1], 45 + s, me, to)
    finish(2)

    for s in range(1, n_seq + 1):
        to = (z + s) % n_seq
        out = lax.dot_general(
            full_attn[tiles(to, cols), :], resid_ref[...], NT, preferred_element_type=f32
        ).astype(bf16)
        if s < n_seq:
            ctx_ref[s - 1] = out
            push(ctx_ref.at[s - 1], dout_ref.at[z], 42 + s, me, to)
        else:
            dout_ref[z] = out

    for s in range(1, n_seq):
        arrive(part_a.at[s - 1], 45 + s)
    mine_a[...] = sums_ref[tiles(z, 8), :] + part_a[0] + part_a[1] + part_a[2]
    for s in range(1, n_dp):
        push(mine_a, part_b.at[me], 48 + s, (me + s) % n_dp, z)
    part_b[me] = mine_a[...]

    for s in range(1, n_seq):
        arrive(dout_ref.at[(z + n_seq - s) % n_seq], 42 + s)

    def attend(first, last):
        @pl.loop(first, last)
        def _(h):
            hd = head(h)
            per = qblock // rows
            for b in range(total // qblock):
                q = pl.ds(b * qblock, qblock)
                probs = probs_ref[h, b]
                dout = jnp.concatenate(
                    [dout_ref[b * per + i, hd, :] for i in range(per)], axis=1
                )
                prob_grad = lax.dot_general(vt_ref[h], dout, NN, preferred_element_type=f32)
                delta = jnp.sum(probs * prob_grad, axis=0, keepdims=True)
                score_grad = (probs * (prob_grad - delta)).astype(bf16)
                value_part = lax.dot_general(dout, probs.astype(bf16), NT, preferred_element_type=f32)
                key_part = lax.dot_general(q_ref[hd, q], score_grad, NT, preferred_element_type=f32)
                query_part = lax.dot_general(k_ref[hd, :], score_grad, NN, preferred_element_type=f32)
                qg_ref[hd, q] = (query_part * scale).astype(bf16)
                if b == 0:
                    va_ref[...] = value_part
                    ka_ref[...] = key_part
                else:
                    va_ref[...] += value_part
                    ka_ref[...] += key_part
            kg_ref[hd, :] = (ka_ref[...] * scale).astype(bf16)
            vg_ref[hd, :] = va_ref[...].astype(bf16)

    attend(0, heads // 2)
    for s in range(1, n_dp):
        arrive(part_b.at[(me + n_dp - s) % n_dp], 48 + s)
    chunk = part_b[0]
    for i in range(1, n_dp):
        chunk = chunk + part_b[i]
    total_ref[tiles(z, 8), :] = chunk
    for s in range(1, n_seq):
        block = total_ref.at[tiles(z, 8), :]
        push(block, block, 55 + s, me, (z + s) % n_seq)
    attend(heads // 2, heads)

    for s in range(1, n_seq):
        arrive(total_ref.at[tiles((z + n_seq - s) % n_seq, 8), :], 55 + s)
    taps_ref[...] = total_ref[0:KW, :]
    gaing_ref[...] = total_ref[KW : KW + 1, :].reshape(width)
    for copy in sent:
        copy.wait_send()


def store_all(*refs):
    sources, targets, sems = refs[:6], refs[6:12], refs[12]
    copies = [
        pltpu.make_async_copy(sources[i], targets[i], sems.at[i]) for i in range(6)
    ]
    for copy in copies:
        copy.start()
    for copy in copies:
        copy.wait()


def fused_local(
    grad_out, saved_input, pre_glu, queries, keys, values, frame_counts, norm_gain, kernel,
    w_in, w_conv_out, w_attn_out,
):
    rows, width = grad_out.shape
    total, cols = queries.shape
    queries, keys, values = queries.T, keys.T, values.T
    heads = cols // HD
    f32, bf16 = jnp.float32, jnp.bfloat16
    vmem = pl.BlockSpec(memory_space=pltpu.VMEM)
    smem = pl.BlockSpec(memory_space=pltpu.SMEM)
    hbm = pl.BlockSpec(memory_space=pltpu.HBM)
    outs = pl.pallas_call(
        fused,
        out_shape=(
            jax.ShapeDtypeStruct((rows, width), bf16),
            jax.ShapeDtypeStruct((cols, total), bf16),
            jax.ShapeDtypeStruct((cols, total), bf16),
            jax.ShapeDtypeStruct((cols, total), bf16),
            jax.ShapeDtypeStruct((KW, width), f32),
            jax.ShapeDtypeStruct((width,), f32),
        ),
        in_specs=[hbm] * 6 + [smem] + [hbm] * 5,
        out_specs=(vmem,) * 6,
        scratch_shapes=[
            pltpu.VMEM((width, width), bf16),
            pltpu.VMEM((width, 2 * width), bf16),
            pltpu.VMEM((width, width), bf16),
            pltpu.VMEM((rows, width), bf16),
            pltpu.VMEM((rows + 32, width), f32),
            pltpu.VMEM((4, 16, width), bf16),
            pltpu.VMEM((rows + 32, LANES), jnp.int32),
            pltpu.VMEM((total, LANES), jnp.int32),
            pltpu.VMEM((KW, rows, LANES), f32),
            pltpu.VMEM((total, HD), bf16),
            pltpu.VMEM((heads, total, HD), bf16),
            pltpu.VMEM((rows, width), f32),
            pltpu.VMEM((rows, width), f32),
            pltpu.VMEM((rows, width), bf16),
            pltpu.VMEM((rows + 32, width), f32),
            pltpu.VMEM((rows, 2 * width), bf16),
            pltpu.VMEM((rows, width), f32),
            pltpu.VMEM((heads, total // 256, total, 256), f32),
            pltpu.VMEM((3, cols, rows), bf16),
            pltpu.VMEM((4, cols, rows), bf16),
            pltpu.VMEM((HD, total), f32),
            pltpu.VMEM((HD, total), f32),
            pltpu.VMEM((KW + 1, width), f32),
            pltpu.VMEM((3, 8, width), f32),
            pltpu.VMEM((8, width), f32),
            pltpu.VMEM((8, 8, width), f32),
            pltpu.VMEM((KW + 1, width), f32),
            pltpu.VMEM((rows, width), bf16),
            pltpu.VMEM((rows, width), bf16),
            pltpu.VMEM((rows, 2 * width), bf16),
            pltpu.VMEM((cols, total), bf16),
            pltpu.VMEM((cols, total), bf16),
            pltpu.VMEM((cols, total), bf16),
            pltpu.VMEM((width,), f32),
            pltpu.VMEM((KW, width), f32),
            pltpu.SemaphoreType.DMA((COPIES,)),
            pltpu.SemaphoreType.DMA((COPIES,)),
            pltpu.SemaphoreType.DMA((11,)),
        ],
        compiler_params=pltpu.CompilerParams(
            collective_id=0, has_side_effects=True, vmem_limit_bytes=63 * 1024 * 1024
        ),
    )(
        grad_out, saved_input, pre_glu, queries, keys, values, frame_counts,
        norm_gain, kernel, w_in, w_conv_out, w_attn_out,
    )
    outs = pl.pallas_call(
        store_all,
        out_shape=tuple(jax.ShapeDtypeStruct(o.shape, o.dtype) for o in outs),
        in_specs=[hbm] * 6,
        out_specs=(hbm,) * 6,
        scratch_shapes=[pltpu.SemaphoreType.DMA((6,))],
        compiler_params=pltpu.CompilerParams(vmem_limit_bytes=63 * 1024 * 1024),
    )(*outs)
    return (outs[0], outs[1].T, outs[2].T, outs[3].T, outs[4], outs[5])


def solution(mesh):
    in_specs = (
        P(("dp", "seq"), None),
        P(("dp", "seq"), None),
        P(("dp", "seq"), None),
        P("dp", "seq"),
        P("dp", "seq"),
        P("dp", "seq"),
        P("dp", None),
        P(),
        P(),
        P("dp", None),
        P("dp", None),
        P("dp", None),
    )
    out_specs = (P(("dp", "seq"), None), P("dp", "seq"), P("dp", "seq"), P("dp", "seq"), P(), P())
    small = mesh.shape["dp"] == 8 and mesh.shape["seq"] == 4
    body = fused_local if small else local
    return jax.shard_map(body, mesh=mesh, in_specs=in_specs, out_specs=out_specs, check_vma=False)
```
